512 devices in a mesh: wide: 64 (over y_hi, z, core), narrow: 8 (over y_lo, x).
Axes of the slice: x: 4, y: 4 (y_hi: 2, y_lo: 2; y = y_hi * 2 + y_lo), z: 16, core: 2. Of those that a mesh axis runs over, the one named last changes fastest.
Arguments:
- descriptors: bfloat16 [1536, 2000], P('narrow'), may hold values from -6 to 6
- env_weights: bfloat16 [1536], P('narrow'), may hold values from 0.19921875 to 5
- sparse_points: bfloat16 [12288, 2000], P(('wide', 'narrow')), may hold values from -6 to 6
Outputs:
- normal: float32 [64, 33, 192, 192], P('wide', None, 'narrow')
The draws below stay inside these ranges and needn't reach their ends.
All inputs are finite; a program needn't handle non-finite values.
Results may differ from the reference program's by a relative error of at most 0.0003.
Values may be sent and summed in bfloat16 or wider, within the bound.
No kernel may reach another device: no remote copies, remote signals or barrier semaphores. Data moves between devices by JAX's collectives and lax.ppermute only.
A program may use at most 64 MiB of HBM per device.

```python
import math
import jax
import jax.numpy as jnp
from jax import lax

W = 2000
ENVS = 1536
M = 12288
N_WIDE = 64


def level_of(rng, shape, cuts, smallest, top_value):
    factor_of, own = 1.0, jax.random.fold_in(rng, 6)
    for dim, parts in cuts:
        draws = jnp.exp(jax.random.uniform(jax.random.fold_in(own, dim), (parts,), jnp.float32, smallest / len(cuts), top_value / len(cuts)))
        factor_of = factor_of * jnp.repeat(draws, shape[dim] // parts).reshape([-1 if axis == dim else 1 for axis in range(len(shape))])
    return factor_of


def centred(rng, extent, scale, most, cuts=(), dtype=jnp.bfloat16):
    factor_of = level_of(rng, extent, cuts, -0.22, 0.18) if cuts else 1.0
    array = jax.random.normal(rng, extent, jnp.float32) * scale * factor_of
    return jnp.minimum(jnp.maximum(array, -most), most).astype(dtype)


def setup_inputs(seed: int = 0) -> dict:
    arg_keys = jax.random.split(jax.random.key(seed), 4)
    descriptors = centred(arg_keys[0], (ENVS, W), 1.0, 6.0, ((0, 8),))
    env_weights = jnp.clip(jnp.exp(math.log(5.0) - 3.2227897 * jax.random.uniform(arg_keys[1], (ENVS,), jnp.float32) ** level_of(arg_keys[1], (ENVS,), ((0, 8),), -0.2, 0.2)), 0.19921875, 5.0).astype(jnp.bfloat16)
    sparse_points = centred(arg_keys[2], (M, W), 1.0, 6.0, ((0, 512),))
    return {"descriptors": descriptors, "env_weights": env_weights, "sparse_points": sparse_points}


def reference(descriptors, env_weights, sparse_points):
    products = jnp.dot(descriptors, sparse_points.T, preferred_element_type=jnp.float32)
    kernel = products * products / W
    weighting = env_weights.astype(jnp.float32) / ENVS
    block_size = sparse_points.shape[0] // N_WIDE
    half_axis = N_WIDE // 2
    kernel_blocks = kernel.reshape(ENVS, N_WIDE, block_size).transpose(1, 0, 2)

    def one_owner(owner):
        weighted = kernel_blocks[owner] * weighting[:, None]
        chosen_ids = ((owner + jnp.arange(half_axis + 1).astype(jnp.int32)) % N_WIDE).astype(jnp.int32)
        chosen = jnp.take(kernel_blocks, chosen_ids, axis=0)
        return jnp.einsum("snb,nc->sbc", chosen, weighted, precision=lax.Precision.HIGHEST)

    return lax.map(one_owner, jnp.arange(N_WIDE).astype(jnp.int32))
```

```python
import jax
import jax.numpy as jnp
from jax import lax
from jax.sharding import PartitionSpec as P


def from_ahead(value, chips):
    size = lax.axis_size("wide")
    return lax.ppermute(value, "wide", [(i, (i - 2 * chips) % size) for i in range(size)])


def from_partner(value):
    size = lax.axis_size("wide")
    return lax.ppermute(value, "wide", [(i, i ^ 1) for i in range(size)])


def squared_dots(left, right, width):
    dots = lax.dot_general(left, right, (((1,), (1,)), ((), ())), preferred_element_type=jnp.float32)
    return dots * dots / width


def pair_blocks(rows, columns):
    return lax.dot_general(
        rows,
        columns,
        (((1,), (0,)), ((), ())),
        precision=lax.Precision.HIGH,
        preferred_element_type=jnp.float32,
    )


def shards(descriptors, env_weights, sparse_points):
    core = lax.axis_index("wide") % 2
    narrow = lax.axis_size("narrow")
    width = descriptors.shape[1]
    half = descriptors.shape[0] // 2
    env_count = descriptors.shape[0] * narrow
    piece = sparse_points.shape[0]
    block = piece * narrow

    points = jnp.pad(sparse_points, ((0, 0), (0, 1)))
    weighted_half = lax.dynamic_slice_in_dim(
        jnp.concatenate([descriptors, env_weights[:, None]], axis=1), core * half, half, 0
    )
    payload, points = lax.optimization_barrier(
        (jnp.concatenate([weighted_half, points], axis=0), points)
    )
    gathered = lax.all_gather(payload, "narrow", axis=0, tiled=False)
    envs = gathered[:, :half].reshape(narrow * half, width + 1)
    block_own = gathered[:, half:].reshape(block, width + 1)
    block_other = from_partner(block_own)

    strided = {0: points}
    for chips in (4, 12, 16, 8):
        strided[chips] = from_ahead(points, chips)

    def bundle(*chips):
        return jnp.concatenate([strided[c] for c in chips], axis=0)

    two_up = from_ahead(bundle(0, 4), 2)
    two_down = from_ahead(bundle(12, 16), -2)
    one_up = from_ahead(bundle(0, 4, 8, 12), 1)
    one_down = from_ahead(bundle(4, 8, 12, 16), -1)
    stride_own = bundle(0, 4, 8, 12, 16)
    twos_own = jnp.concatenate([two_up, two_down], axis=0)

    def in_order(stride, twos, ups, downs):
        cut = lambda rows, j: rows[j * piece : (j + 1) * piece]
        parts = []
        for j in range(17):
            source, index = ((stride, j // 4), (ups, j // 4), (twos, j // 4), (downs, j // 4))[j % 4]
            parts.append(cut(source, index))
        return jnp.concatenate(parts, axis=0)

    own = in_order(stride_own, twos_own, one_up, one_down)
    other = in_order(*(from_partner(v) for v in (stride_own, twos_own, one_up, one_down)))

    kernel_own = squared_dots(own, envs, width)
    kernel_other = squared_dots(other, envs, width)
    scale = envs[:, width:].astype(jnp.float32) / env_count
    columns_own = squared_dots(envs, block_own, width) * scale
    columns_other = squared_dots(envs, block_other, width) * scale

    odd = 16 * piece
    rows_other = jnp.concatenate(
        [kernel_other, lax.dynamic_slice_in_dim(kernel_own, (1 - core) * piece, odd, 0)], axis=0
    )
    arrived = from_partner(pair_blocks(rows_other, columns_other))
    rows_own = jnp.concatenate(
        [kernel_own, lax.dynamic_slice_in_dim(kernel_other, core * piece, odd, 0)], axis=0
    )
    total = (pair_blocks(rows_own, columns_own) + arrived).reshape(33, piece, block)
    even, odds = total[:17], total[17:]
    mixed = jnp.stack([even[:16], odds], axis=1).reshape(32, piece, block)
    return jnp.concatenate([mixed, even[16:]], axis=0)[None]


def solution(mesh):
    in_specs = (P("narrow", None), P("narrow"), P(("wide", "narrow"), None))
    out_specs = P("wide", None, "narrow", None)
    return jax.shard_map(shards, mesh=mesh, in_specs=in_specs, out_specs=out_specs, check_vma=False)
```

```python
import functools

import jax
import jax.numpy as jnp
from jax import lax
from jax.experimental import pallas as pl
from jax.experimental.pallas import tpu as pltpu
from jax.sharding import PartitionSpec as P

LANES = 2048
UNITS = (
    (0, True), (4, True), (8, True), (12, False), (16, True),
    (1, True), (5, True), (9, True), (13, False),
    (15, False), (11, False), (7, False), (3, True),
    (2, True), (6, True), (14, False), (10, False),
)


def permuted(value, move):
    wide, narrow = lax.axis_size("wide"), lax.axis_size("narrow")
    pairs = []
    for w in range(wide):
        for n in range(narrow):
            to_w, to_n = move(w, n)
            pairs.append((w * narrow + n, (to_w % wide) * narrow + to_n % narrow))
    return lax.ppermute(value, ("wide", "narrow"), pairs)


def by_chips(value, first, second):
    return permuted(value, lambda w, n: (w + 2 * (second if w % 2 else first), n))


def from_partner(value):
    return permuted(value, lambda w, n: (w ^ 1, n))


def gather_wide(unit, core, piece):
    four = by_chips(unit, -4, -12)
    across = by_chips(unit[:piece], -16, -16)
    eight = by_chips(four[:piece], -4, 4)
    got = from_partner(jnp.concatenate([four, eight, across], axis=0))
    sixteen = jnp.concatenate([across, got[3 * piece :]], axis=0)
    start = jnp.where(core == 0, unit, sixteen)
    stop = jnp.where(core == 0, sixteen, unit)
    bundle = jnp.concatenate([start, four, eight, got[2 * piece : 3 * piece], got[: 2 * piece]], axis=0)
    near = by_chips(bundle, -1, 1)
    two = by_chips(near[: 4 * piece], -1, 1)
    far = from_partner(near)
    two_far = from_partner(two)
    return bundle, stop, near, far, two, two_far


def products_kernel(piece, shards_x, rows_d, tile, width, env_count, *refs):
    gathered, points = refs[0], refs[1:7]
    own_ref, send_ref = refs[7:9]
    envs, rows, dots, columns, own, send, sems = refs[9:]
    count = len(UNITS) * 2 * piece
    block = 2 * shards_x * piece

    copies, at = [], 0
    for ref in points:
        size = ref.shape[0]
        copies.append(pltpu.make_async_copy(ref, rows.at[pl.ds(at, size)], sems.at[len(copies)]))
        at += size
    for i in range(shards_x):
        copies.append(
            pltpu.make_async_copy(
                gathered.at[i, pl.ds(rows_d, 4 * piece)],
                rows.at[pl.ds(at, 4 * piece)],
                sems.at[len(copies)],
            )
        )
        at += 4 * piece
    for i in range(shards_x):
        copies.append(
            pltpu.make_async_copy(
                gathered.at[i, pl.ds(0, rows_d)], envs.at[pl.ds(i * rows_d, rows_d)], sems.at[len(copies)]
            )
        )
    for copy in copies:
        copy.start()
    pick = (lax.broadcasted_iota(jnp.int32, (16, LANES), 1) == width) & (
        lax.broadcasted_iota(jnp.int32, (16, LANES), 0) == 0
    )
    rows[pl.ds(at, 16), :] = pick.astype(jnp.float32).astype(jnp.bfloat16)
    for copy in copies:
        copy.wait()

    total = rows.shape[0]
    step = total // 4
    for t in range(envs.shape[0] // tile):
        def some_dots(m, carry):
            part = pl.ds(pl.multiple_of(m * step, 16), step)
            dots[part, :] = lax.dot_general(
                rows[part, :],
                envs[pl.ds(t * tile, tile), :],
                (((1,), (1,)), ((), ())),
                preferred_element_type=jnp.float32,
            )
            return carry

        lax.fori_loop(0, 4, some_dots, 0)
        weights = dots[pl.ds(at, 8), :][:1] / env_count
        for i in range(shards_x):
            for which in range(2):
                for low in range(2):
                    source = count + i * 4 * piece + (2 * which + low) * piece
                    target = which * block + (low * shards_x + i) * piece
                    value = dots[pl.ds(source, piece), :]
                    columns[pl.ds(target, piece), :] = value * value / width * weights
        high, low_part = [], []
        for which in range(2):
            value = columns[pl.ds(which * block, block), :]
            top = value.astype(jnp.bfloat16)
            high.append(top)
            low_part.append((value - top.astype(jnp.float32)).astype(jnp.bfloat16))

        def some_products(m, carry):
            part = pl.ds(pl.multiple_of(m * (count // 3), 8), count // 3)
            value = dots[part, :]
            value = value * value / width
            top = value.astype(jnp.bfloat16)
            rest = (value - top.astype(jnp.float32)).astype(jnp.bfloat16)
            for which, target in ((0, own), (1, send)):
                result = 0
                for left, right in ((top, high[which]), (top, low_part[which]), (rest, high[which])):
                    result += lax.dot_general(
                        left, right, (((1,), (1,)), ((), ())), preferred_element_type=jnp.float32
                    )
                target[part, :] = result if t == 0 else target[part, :] + result
            return carry

        lax.fori_loop(0, 3, some_products, 0)

    for u, (distance, first_own) in enumerate(UNITS):
        for b in range(2):
            part = pl.ds((2 * u + b) * piece, piece)
            if first_own == (b == 0):
                own_ref[2 * distance] = own[part, :]
                if distance > 0:
                    send_ref[33 - 2 * distance] = send[part, :]
            else:
                if distance < 16:
                    own_ref[2 * distance + 1] = own[part, :]
                send_ref[32 - 2 * distance] = send[part, :]


def products(gathered, points, piece, rows_d, width, env_count):
    shards_x = gathered.shape[0]
    env_rows = shards_x * rows_d
    tile = 256 if env_rows % 256 == 0 else env_rows
    count = len(UNITS) * 2 * piece
    block = 2 * shards_x * piece
    total = count + 4 * shards_x * piece + 16
    shape = jax.ShapeDtypeStruct((33, piece, block), jnp.float32)
    anywhere = pl.BlockSpec(memory_space=pl.ANY)
    vmem = pl.BlockSpec(memory_space=pltpu.VMEM)
    flops = 2 * env_rows * (total * LANES + 6 * count * block)
    return pl.pallas_call(
        functools.partial(products_kernel, piece, shards_x, rows_d, tile, width, env_count),
        out_shape=(shape, shape),
        in_specs=[anywhere] * (1 + len(points)),
        out_specs=(vmem, vmem),
        scratch_shapes=[
            pltpu.VMEM((env_rows, LANES), jnp.bfloat16),
            pltpu.VMEM((total, LANES), jnp.bfloat16),
            pltpu.VMEM((total, tile), jnp.float32),
            pltpu.VMEM((2 * block, tile), jnp.float32),
            pltpu.VMEM((count, block), jnp.float32),
            pltpu.VMEM((count, block), jnp.float32),
            pltpu.SemaphoreType.DMA((len(points) + 2 * shards_x,)),
        ],
        compiler_params=pltpu.CompilerParams(vmem_limit_bytes=40 * 1024 * 1024),
        cost_estimate=pl.CostEstimate(flops=flops, bytes_accessed=10**7, transcendentals=0),
    )(gathered, *points)


def shards(descriptors, env_weights, sparse_points):
    core = lax.axis_index("wide") % 2
    narrow = lax.axis_size("narrow")
    wide = lax.axis_size("wide")
    shards_x = narrow // 2
    width = descriptors.shape[1]
    half = descriptors.shape[0] // 2
    env_count = descriptors.shape[0] * narrow
    piece = sparse_points.shape[0]

    mine = jnp.pad(sparse_points, ((0, 0), (0, LANES - width)))
    other = from_partner(mine)
    half_envs = lax.dynamic_slice_in_dim(
        jnp.concatenate(
            [descriptors, env_weights[:, None], jnp.zeros((2 * half, LANES - width - 1), descriptors.dtype)], axis=1
        ),
        core * half,
        half,
        0,
    )
    across_envs = permuted(
        half_envs, lambda w, n: (w + (wide // 2 if w % 2 else 0), n + shards_x)
    )
    unit = jnp.concatenate([mine, other], axis=0)
    across_unit = permuted(unit, lambda w, n: (w, n + shards_x))
    at_zero = lax.axis_index("narrow") < shards_x
    low = jnp.where(at_zero, unit, across_unit)
    high = jnp.where(at_zero, across_unit, unit)
    payload = jnp.concatenate(
        [half_envs, across_envs, low[:piece], high[:piece], low[piece:], high[piece:]], axis=0
    )
    payload, unit = lax.optimization_barrier((payload, unit))
    groups = [list(range(shards_x)), list(range(shards_x, narrow))]
    gathered = lax.all_gather(payload, "narrow", axis=0, tiled=False, axis_index_groups=groups)

    def none(_):
        return tuple(jnp.zeros((n * piece, LANES), unit.dtype) for n in (8, 2, 8, 8, 4, 4))

    points = lax.cond(
        1 + jnp.minimum(lax.axis_index("wide"), 0) > 0,
        lambda value: gather_wide(value, core, piece),
        none,
        unit,
    )
    gathered, points = lax.optimization_barrier((gathered, points))
    kept, sent = products(gathered, points, piece, 2 * half, width, env_count)
    total = kept + from_partner(sent)
    return jnp.where(core == 0, total, total[::-1])[None]


def solution(mesh):
    in_specs = (P("narrow", None), P("narrow"), P(("wide", "narrow"), None))
    out_specs = P("wide", None, "narrow", None)
    return jax.shard_map(shards, mesh=mesh, in_specs=in_specs, out_specs=out_specs, check_vma=False)
```

```python
import functools

import jax
import jax.numpy as jnp
from jax import lax
from jax.experimental import pallas as pl
from jax.experimental.pallas import tpu as pltpu
from jax.sharding import PartitionSpec as P

LANES = 2048
UNITS = (
    (0, True), (4, True), (8, True), (12, False), (16, True),
    (1, True), (5, True), (9, True), (13, False),
    (15, False), (11, False), (7, False), (3, True),
    (2, True), (6, True), (14, False), (10, False),
)


def permuted(value, move):
    wide, narrow = lax.axis_size("wide"), lax.axis_size("narrow")
    pairs = []
    for w in range(wide):
        for n in range(narrow):
            to_w, to_n = move(w, n)
            pairs.append((w * narrow + n, (to_w % wide) * narrow + to_n % narrow))
    return lax.ppermute(value, ("wide", "narrow"), pairs)


def by_chips(value, first, second):
    return permuted(value, lambda w, n: (w + 2 * (second if w % 2 else first), n))


def from_partner(value):
    return permuted(value, lambda w, n: (w ^ 1, n))


def gather_wide(unit, sixteen_mine, core, piece):
    four = by_chips(unit, -4, -12)
    sixteen = jnp.concatenate([sixteen_mine, from_partner(sixteen_mine)], axis=0)
    start = jnp.where(core == 0, unit, sixteen)
    stop = jnp.where(core == 0, sixteen, unit)
    eight = by_chips(four[:piece], -4, 4)
    near = by_chips(jnp.concatenate([start, four], axis=0), -1, 1)
    got = from_partner(jnp.concatenate([four, eight], axis=0))
    two = by_chips(near, -1, 1)
    eights = jnp.concatenate([eight, got[2 * piece :]], axis=0)
    twelve = got[: 2 * piece]
    near_late = by_chips(jnp.concatenate([eights, twelve], axis=0), -1, 1)
    far = from_partner(near)
    two_far = from_partner(two)
    far_late = from_partner(near_late)
    return start, four, eights, twelve, stop, near, near_late, far, far_late, two, two_far


def products_kernel(piece, shards_x, rows_d, tile, width, env_count, *refs):
    gathered, points = refs[0], refs[1:12]
    own_ref, send_ref = refs[12:14]
    envs, rows, dots, columns, own, send, sems = refs[14:]
    count = len(UNITS) * 2 * piece
    block = 2 * shards_x * piece
    at = count + 4 * shards_x * piece
    tiles = envs.shape[0] // tile

    def copied(source, target):
        copies.append(pltpu.make_async_copy(source, target, sems.at[len(copies)]))
        copies[-1].start()
        return copies[-1]

    def copied_envs(i):
        return copied(gathered.at[i, pl.ds(0, rows_d)], envs.at[pl.ds(i * rows_d, rows_d)])

    copies, row_copies, sizes = [], [], []
    first = -(-tile // rows_d)
    env_copies = [copied_envs(i) for i in range(first)]
    place = 0
    for group in ((0, 1, 2, 3, 4), (5, 6), (7, 8), (9, 10)):
        row_copies.append([])
        begin = place
        for k in group:
            size = points[k].shape[0]
            row_copies[-1].append(copied(points[k], rows.at[pl.ds(place, size)]))
            place += size
        sizes.append(place - begin)
    row_copies.append([])
    for i in range(shards_x):
        row_copies[-1].append(
            copied(gathered.at[i, pl.ds(rows_d, 4 * piece)], rows.at[pl.ds(place, 4 * piece)])
        )
        place += 4 * piece
    sizes.append(4 * shards_x * piece + 16)
    late_copies = [copied_envs(i) for i in range(first, shards_x)]
    pick = (lax.broadcasted_iota(jnp.int32, (16, LANES), 1) == width) & (
        lax.broadcasted_iota(jnp.int32, (16, LANES), 0) == 0
    )
    rows[pl.ds(at, 16), :] = pick.astype(jnp.float32).astype(jnp.bfloat16)

    def dots_of(part, t):
        dots[part, :] = lax.dot_general(
            rows[part, :],
            envs[pl.ds(t * tile, tile), :],
            (((1,), (1,)), ((), ())),
            preferred_element_type=jnp.float32,
        )

    step = rows.shape[0] // 4
    for t in range(tiles):
        if t == 0:
            for copy in env_copies:
                copy.wait()
            place = 0
            for waits, size in zip(row_copies, sizes):
                for copy in waits:
                    copy.wait()
                dots_of(pl.ds(place, size), 0)
                place += size
            for copy in late_copies:
                copy.wait()
        else:
            def some_dots(m, carry):
                dots_of(pl.ds(pl.multiple_of(m * step, 16), step), t)
                return carry

            lax.fori_loop(0, 4, some_dots, 0)
        weights = dots[pl.ds(at, 8), :][:1] / env_count
        for i in range(shards_x):
            for which in range(2):
                for low in range(2):
                    source = count + i * 4 * piece + (2 * which + low) * piece
                    target = which * block + (low * shards_x + i) * piece
                    value = dots[pl.ds(source, piece), :]
                    columns[pl.ds(target, piece), :] = value * value / width * weights
        high, low_part = [], []
        for which in range(2):
            value = columns[pl.ds(which * block, block), :]
            top = value.astype(jnp.bfloat16)
            high.append(top)
            low_part.append((value - top.astype(jnp.float32)).astype(jnp.bfloat16))

        def some_products(m, carry):
            part = pl.ds(pl.multiple_of(m * (count // 3), 8), count // 3)
            value = dots[part, :]
            value = value * value / width
            top = value.astype(jnp.bfloat16)
            rest = (value - top.astype(jnp.float32)).astype(jnp.bfloat16)
            for which, target in ((0, own), (1, send)):
                result = 0
                for left, right in ((top, high[which]), (top, low_part[which]), (rest, high[which])):
                    result += lax.dot_general(
                        left, right, (((1,), (1,)), ((), ())), preferred_element_type=jnp.float32
                    )
                target[part, :] = result if t == 0 else target[part, :] + result
            return carry

        lax.fori_loop(0, 3, some_products, 0)

    for u, (distance, first_own) in enumerate(UNITS):
        for b in range(2):
            part = pl.ds((2 * u + b) * piece, piece)
            if first_own == (b == 0):
                own_ref[2 * distance] = own[part, :]
                if distance > 0:
                    send_ref[33 - 2 * distance] = send[part, :]
            else:
                if distance < 16:
                    own_ref[2 * distance + 1] = own[part, :]
                send_ref[32 - 2 * distance] = send[part, :]


def products(gathered, points, piece, rows_d, width, env_count):
    shards_x = gathered.shape[0]
    env_rows = shards_x * rows_d
    tile = 256 if env_rows % 256 == 0 else env_rows
    count = len(UNITS) * 2 * piece
    block = 2 * shards_x * piece
    total = count + 4 * shards_x * piece + 16
    shape = jax.ShapeDtypeStruct((33, piece, block), jnp.float32)
    anywhere = pl.BlockSpec(memory_space=pl.ANY)
    vmem = pl.BlockSpec(memory_space=pltpu.VMEM)
    flops = 2 * env_rows * (total * LANES + 6 * count * block)
    return pl.pallas_call(
        functools.partial(products_kernel, piece, shards_x, rows_d, tile, width, env_count),
        out_shape=(shape, shape),
        in_specs=[anywhere] * (1 + len(points)),
        out_specs=(vmem, vmem),
        scratch_shapes=[
            pltpu.VMEM((env_rows, LANES), jnp.bfloat16),
            pltpu.VMEM((total, LANES), jnp.bfloat16),
            pltpu.VMEM((total, tile), jnp.float32),
            pltpu.VMEM((2 * block, tile), jnp.float32),
            pltpu.VMEM((count, block), jnp.float32),
            pltpu.VMEM((count, block), jnp.float32),
            pltpu.SemaphoreType.DMA((len(points) + 2 * shards_x,)),
        ],
        compiler_params=pltpu.CompilerParams(vmem_limit_bytes=60 * 1024 * 1024),
        cost_estimate=pl.CostEstimate(flops=flops, bytes_accessed=10**7, transcendentals=0),
    )(gathered, *points)


def shards(descriptors, env_weights, sparse_points):
    core = lax.axis_index("wide") % 2
    narrow = lax.axis_size("narrow")
    wide = lax.axis_size("wide")
    shards_x = narrow // 2
    width = descriptors.shape[1]
    half = descriptors.shape[0] // 2
    env_count = descriptors.shape[0] * narrow
    piece = sparse_points.shape[0]

    mine = jnp.pad(sparse_points, ((0, 0), (0, LANES - width)))
    other = from_partner(mine)
    across_mine = permuted(mine, lambda w, n: (w, n + shards_x))
    unit = jnp.concatenate([mine, other], axis=0)
    half_envs = lax.dynamic_slice_in_dim(
        jnp.concatenate(
            [descriptors, env_weights[:, None], jnp.zeros((2 * half, LANES - width - 1), descriptors.dtype)], axis=1
        ),
        core * half,
        half,
        0,
    )
    across_envs = permuted(
        half_envs, lambda w, n: (w + (wide // 2 if w % 2 else 0), n + shards_x)
    )
    across_other = from_partner(across_mine)
    sixteen_mine = by_chips(mine, -16, -16)
    at_zero = lax.axis_index("narrow") < shards_x
    payload = jnp.concatenate(
        [
            half_envs,
            across_envs,
            jnp.where(at_zero, mine, across_mine),
            jnp.where(at_zero, across_mine, mine),
            jnp.where(at_zero, other, across_other),
            jnp.where(at_zero, across_other, other),
        ],
        axis=0,
    )
    payload, unit, sixteen_mine = lax.optimization_barrier((payload, unit, sixteen_mine))
    groups = [list(range(shards_x)), list(range(shards_x, narrow))]
    gathered = lax.all_gather(payload, "narrow", axis=0, tiled=False, axis_index_groups=groups)

    def none(*_):
        return tuple(jnp.zeros((n * piece, LANES), unit.dtype) for n in (2, 2, 2, 2, 2, 4, 4, 4, 4, 4, 4))

    points = lax.cond(
        1 + jnp.minimum(lax.axis_index("wide"), 0) > 0,
        lambda *values: gather_wide(*values, core, piece),
        none,
        unit,
        sixteen_mine,
    )
    gathered, points = lax.optimization_barrier((gathered, points))
    kept, sent = products(gathered, points, piece, 2 * half, width, env_count)
    total = kept + from_partner(sent)
    return jnp.where(core == 0, total, total[::-1])[None]


def solution(mesh):
    in_specs = (P("narrow", None), P("narrow"), P(("wide", "narrow"), None))
    out_specs = P("wide", None, "narrow", None)
    return jax.shard_map(shards, mesh=mesh, in_specs=in_specs, out_specs=out_specs, check_vma=False)
```

```python
import functools

import jax
import jax.numpy as jnp
from jax import lax
from jax.experimental import pallas as pl
from jax.experimental.pallas import tpu as pltpu
from jax.sharding import PartitionSpec as P

LANES = 2048
UNITS = (
    (0, True), (4, True), (8, True), (12, False), (16, True),
    (1, True), (5, True), (9, True), (13, False),
    (15, False), (11, False), (7, False), (3, True),
    (2, True), (6, True), (14, False), (10, False),
)


def permuted(value, move):
    wide, narrow = lax.axis_size("wide"), lax.axis_size("narrow")
    pairs = []
    for w in range(wide):
        for n in range(narrow):
            to_w, to_n = move(w, n)
            pairs.append((w * narrow + n, (to_w % wide) * narrow + to_n % narrow))
    return lax.ppermute(value, ("wide", "narrow"), pairs)


def by_chips(value, first, second):
    return permuted(value, lambda w, n: (w + 2 * (second if w % 2 else first), n))


def from_partner(value):
    return permuted(value, lambda w, n: (w ^ 1, n))


def gather_wide(unit, four_mine, core, piece):
    eight = by_chips(four_mine, -4, 4)
    four = jnp.concatenate([four_mine, by_chips(unit[piece:], -4, -12)], axis=0)
    sixteen_mine = by_chips(unit[:piece], -16, -16)
    sixteen = jnp.concatenate([sixteen_mine, from_partner(sixteen_mine)], axis=0)
    start = jnp.where(core == 0, unit, sixteen)
    stop = jnp.where(core == 0, sixteen, unit)
    near = by_chips(jnp.concatenate([start, four], axis=0), -1, 1)
    got = from_partner(jnp.concatenate([four, eight], axis=0))
    two = by_chips(near, -1, 1)
    eights = jnp.concatenate([eight, got[2 * piece :]], axis=0)
    twelve = got[: 2 * piece]
    near_late = by_chips(jnp.concatenate([eights, twelve], axis=0), -1, 1)
    far = from_partner(near)
    two_far = from_partner(two)
    far_late = from_partner(near_late)
    return start, four, eights, twelve, stop, near, near_late, far, far_late, two, two_far


def dots_of(rows, envs):
    return lax.dot_general(rows, envs, (((1,), (1,)), ((), ())), preferred_element_type=jnp.float32)


def two_parts(value):
    top = value.astype(jnp.bfloat16)
    return top, (value - top.astype(jnp.float32)).astype(jnp.bfloat16)


def rows_kernel(shards_x, rows_d, tile, width, *refs):
    gathered, points = refs[0], refs[1:12]
    high_ref, low_ref = refs[12:14]
    envs, rows, sems = refs[14:]
    copies = []

    def copied(source, target):
        copies.append(pltpu.make_async_copy(source, target, sems.at[len(copies)]))
        copies[-1].start()
        return copies[-1]

    def copied_envs(i):
        return copied(gathered.at[i, pl.ds(0, rows_d)], envs.at[pl.ds(i * rows_d, rows_d)])

    first = -(-tile // rows_d)
    env_copies = [copied_envs(i) for i in range(first)]
    row_copies, sizes, place = [], [], 0
    for group in ((0, 1, 2, 3, 4), (5, 6), (7, 8), (9, 10)):
        row_copies.append([])
        begin = place
        for k in group:
            size = points[k].shape[0]
            row_copies[-1].append(copied(points[k], rows.at[pl.ds(place, size)]))
            place += size
        sizes.append(place - begin)
    late_copies = [copied_envs(i) for i in range(first, shards_x)]

    def some(part, t):
        value = dots_of(rows[part, :], envs[pl.ds(t * tile, tile), :])
        top, rest = two_parts(value * value / width)
        high_ref[part, pl.ds(t * tile, tile)] = top
        low_ref[part, pl.ds(t * tile, tile)] = rest

    for copy in env_copies:
        copy.wait()
    place = 0
    for waits, size in zip(row_copies, sizes):
        for copy in waits:
            copy.wait()
        some(pl.ds(place, size), 0)
        place += size
    for copy in late_copies:
        copy.wait()
    step = place // 3
    for t in range(1, envs.shape[0] // tile):
        def body(m, carry):
            some(pl.ds(pl.multiple_of(m * step, 16), step), t)
            return carry

        lax.fori_loop(0, 3, body, 0)


def products_kernel(piece, shards_x, rows_d, tile, width, env_count, core_ref, *refs):
    gathered, other, high_ref, low_ref = refs[:4]
    own_ref, send_ref = refs[4:6]
    envs, rows, dots, columns, own, send, sems = refs[6:]
    count = len(UNITS) * 2 * piece
    block = 2 * shards_x * piece
    at = 2 * block
    copies = []

    def copied(source, target):
        copies.append(pltpu.make_async_copy(source, target, sems.at[len(copies)]))
        copies[-1].start()
        return copies[-1]

    def copied_envs(i):
        return copied(gathered.at[i, pl.ds(0, rows_d)], envs.at[pl.ds(i * rows_d, rows_d)])

    first = -(-tile // rows_d)
    waits = [copied_envs(i) for i in range(first)]
    for i in range(shards_x):
        waits.append(copied(gathered.at[i, pl.ds(rows_d, 2 * piece)], rows.at[pl.ds(2 * i * piece, 2 * piece)]))
    waits.append(copied(other, rows.at[pl.ds(block, block)]))
    late = [copied_envs(i) for i in range(first, shards_x)]
    pick = (lax.broadcasted_iota(jnp.int32, (16, LANES), 1) == width) & (
        lax.broadcasted_iota(jnp.int32, (16, LANES), 0) == 0
    )
    rows[pl.ds(at, 16), :] = pick.astype(jnp.float32).astype(jnp.bfloat16)
    for copy in waits:
        copy.wait()

    for t in range(envs.shape[0] // tile):
        lanes = pl.ds(t * tile, tile)
        dots[...] = dots_of(rows[...], envs[lanes, :])
        if t == 0:
            for copy in late:
                copy.wait()
        weights = dots[pl.ds(at, 8), :][:1] / env_count
        for which in range(2):
            for i in range(shards_x):
                for low in range(2):
                    source = which * block + (2 * i + low) * piece
                    target = which * block + (low * shards_x + i) * piece
                    value = dots[pl.ds(source, piece), :]
                    columns[pl.ds(target, piece), :] = value * value / width * weights
        parts = [two_parts(columns[pl.ds(which * block, block), :]) for which in range(2)]

        def some_products(m, carry):
            part = pl.ds(pl.multiple_of(m * (count // 3), 16), count // 3)
            top, rest = high_ref[part, lanes], low_ref[part, lanes]
            for which, target in ((0, own), (1, send)):
                high, low_part = parts[which]
                result = dots_of(top, high) + dots_of(top, low_part) + dots_of(rest, high)
                target[part, :] = result if t == 0 else target[part, :] + result
            return carry

        lax.fori_loop(0, 3, some_products, 0)

    core = core_ref[0]
    for u, (distance, first_own) in enumerate(UNITS):
        for b in range(2):
            part = pl.ds((2 * u + b) * piece, piece)
            mine = first_own == (b == 0)
            near = 2 * distance + (0 if mine else 1)
            away = (33 if mine else 32) - 2 * distance
            if near < 33:
                own_ref[near + core * (32 - 2 * near)] = own[part, :]
            if away < 33:
                send_ref[away + (1 - core) * (32 - 2 * away)] = send[part, :]


def tile_of(env_rows):
    return 256 if env_rows % 256 == 0 else env_rows


def rows_call(gathered, points, rows_d, width):
    shards_x = gathered.shape[0]
    env_rows = shards_x * rows_d
    count = sum(p.shape[0] for p in points)
    shape = jax.ShapeDtypeStruct((count, env_rows), jnp.bfloat16)
    vmem = pl.BlockSpec(memory_space=pltpu.VMEM)
    return pl.pallas_call(
        functools.partial(rows_kernel, shards_x, rows_d, tile_of(env_rows), width),
        out_shape=(shape, shape),
        in_specs=[pl.BlockSpec(memory_space=pltpu.HBM)] + [pl.BlockSpec(memory_space=pl.ANY)] * len(points),
        out_specs=(vmem, vmem),
        scratch_shapes=[
            pltpu.VMEM((env_rows, LANES), jnp.bfloat16),
            pltpu.VMEM((count, LANES), jnp.bfloat16),
            pltpu.SemaphoreType.DMA((len(points) + shards_x,)),
        ],
        compiler_params=pltpu.CompilerParams(vmem_limit_bytes=24 * 1024 * 1024),
        cost_estimate=pl.CostEstimate(
            flops=2 * env_rows * count * LANES, bytes_accessed=9 * 10**6, transcendentals=0
        ),
    )(gathered, *points)


def products_call(core, gathered, other, high, low, piece, rows_d, width, env_count):
    shards_x = gathered.shape[0]
    env_rows = shards_x * rows_d
    tile = tile_of(env_rows)
    count = high.shape[0]
    block = 2 * shards_x * piece
    shape = jax.ShapeDtypeStruct((33, piece, block), jnp.float32)
    vmem = pl.BlockSpec(memory_space=pltpu.VMEM)
    return pl.pallas_call(
        functools.partial(products_kernel, piece, shards_x, rows_d, tile, width, env_count),
        out_shape=(shape, shape),
        in_specs=[
            pl.BlockSpec(memory_space=pltpu.SMEM),
            pl.BlockSpec(memory_space=pltpu.HBM),
            pl.BlockSpec(memory_space=pl.ANY),
            vmem,
            vmem,
        ],
        out_specs=(vmem, vmem),
        scratch_shapes=[
            pltpu.VMEM((env_rows, LANES), jnp.bfloat16),
            pltpu.VMEM((2 * block + 16, LANES), jnp.bfloat16),
            pltpu.VMEM((2 * block + 16, tile), jnp.float32),
            pltpu.VMEM((2 * block, tile), jnp.float32),
            pltpu.VMEM((count, block), jnp.float32),
            pltpu.VMEM((count, block), jnp.float32),
            pltpu.SemaphoreType.DMA((1 + 2 * shards_x,)),
        ],
        compiler_params=pltpu.CompilerParams(vmem_limit_bytes=24 * 1024 * 1024),
        cost_estimate=pl.CostEstimate(
            flops=2 * env_rows * (2 * block * LANES + 6 * count * block), bytes_accessed=9 * 10**6, transcendentals=0
        ),
    )(core, gathered, other, high, low)


def shards(descriptors, env_weights, sparse_points):
    core = lax.axis_index("wide") % 2
    narrow = lax.axis_size("narrow")
    wide = lax.axis_size("wide")
    shards_x = narrow // 2
    width = descriptors.shape[1]
    half = descriptors.shape[0] // 2
    env_count = descriptors.shape[0] * narrow
    piece = sparse_points.shape[0]

    mine = jnp.pad(sparse_points, ((0, 0), (0, LANES - width)))
    other = from_partner(mine)
    across_mine = permuted(mine, lambda w, n: (w, n + shards_x))
    unit = jnp.concatenate([mine, other], axis=0)
    half_envs = lax.dynamic_slice_in_dim(
        jnp.concatenate(
            [descriptors, env_weights[:, None], jnp.zeros((2 * half, LANES - width - 1), descriptors.dtype)], axis=1
        ),
        core * half,
        half,
        0,
    )
    across_envs = permuted(
        half_envs, lambda w, n: (w + (wide // 2 if w % 2 else 0), n + shards_x)
    )
    four_mine = by_chips(mine, -4, -12)
    at_zero = lax.axis_index("narrow") < shards_x
    payload = jnp.concatenate(
        [
            half_envs,
            across_envs,
            jnp.where(at_zero, mine, across_mine),
            jnp.where(at_zero, across_mine, mine),
        ],
        axis=0,
    )
    payload, unit, four_mine = lax.optimization_barrier((payload, unit, four_mine))
    groups = [list(range(shards_x)), list(range(shards_x, narrow))]
    gathered = lax.all_gather(payload, "narrow", axis=0, tiled=False, axis_index_groups=groups)

    def none(*_):
        return tuple(jnp.zeros((n * piece, LANES), unit.dtype) for n in (2, 2, 2, 2, 2, 4, 4, 4, 4, 4, 4))

    points = lax.cond(
        1 + jnp.minimum(lax.axis_index("wide"), 0) > 0,
        lambda *values: gather_wide(*values, core, piece),
        none,
        unit,
        four_mine,
    )
    gathered, points = lax.optimization_barrier((gathered, points))
    block_other = from_partner(gathered[:, 2 * half :].reshape(-1, LANES))
    high, low = rows_call(gathered, points, 2 * half, width)
    kept, sent = products_call(
        core.reshape(1), gathered, block_other, high, low, piece, 2 * half, width, env_count
    )
    return (kept + from_partner(sent))[None]


def solution(mesh):
    in_specs = (P("narrow", None), P("narrow"), P(("wide", "narrow"), None))
    out_specs = P("wide", None, "narrow", None)
    return jax.shard_map(shards, mesh=mesh, in_specs=in_specs, out_specs=out_specs, check_vma=False)
```

```python
import functools

import jax
import jax.numpy as jnp
from jax import lax
from jax.experimental import pallas as pl
from jax.experimental.pallas import tpu as pltpu
from jax.sharding import PartitionSpec as P

LANES = 2048
UNITS = (
    (0, True), (4, True), (8, True), (12, False), (16, True),
    (1, True), (5, True), (9, True), (13, False),
    (15, False), (11, False), (7, False), (3, True),
    (2, True), (6, True), (14, False), (10, False),
)


def permuted(value, move):
    wide, narrow = lax.axis_size("wide"), lax.axis_size("narrow")
    pairs = []
    for w in range(wide):
        for n in range(narrow):
            to_w, to_n = move(w, n)
            pairs.append((w * narrow + n, (to_w % wide) * narrow + to_n % narrow))
    return lax.ppermute(value, ("wide", "narrow"), pairs)


def by_chips(value, first, second):
    return permuted(value, lambda w, n: (w + 2 * (second if w % 2 else first), n))


def from_partner(value):
    return permuted(value, lambda w, n: (w ^ 1, n))


def gather_wide(unit, four_mine, core, piece):
    eight = by_chips(four_mine, -4, 4)
    four = jnp.concatenate([four_mine, by_chips(unit[piece:], -4, -12)], axis=0)
    sixteen_mine = by_chips(unit[:piece], -16, -16)
    sixteen = jnp.concatenate([sixteen_mine, from_partner(sixteen_mine)], axis=0)
    start = jnp.where(core == 0, unit, sixteen)
    stop = jnp.where(core == 0, sixteen, unit)
    near = by_chips(jnp.concatenate([start, four], axis=0), -1, 1)
    got = from_partner(jnp.concatenate([four, eight], axis=0))
    two = by_chips(near, -1, 1)
    eights = jnp.concatenate([eight, got[2 * piece :]], axis=0)
    twelve = got[: 2 * piece]
    near_late = by_chips(jnp.concatenate([eights, twelve], axis=0), -1, 1)
    far = from_partner(near)
    two_far = from_partner(two)
    far_late = from_partner(near_late)
    return start, four, eights, twelve, stop, near, near_late, far, far_late, two, two_far


def dots_of(rows, envs):
    return lax.dot_general(rows, envs, (((1,), (1,)), ((), ())), preferred_element_type=jnp.float32)


def two_parts(value):
    top = value.astype(jnp.bfloat16)
    return top, (value - top.astype(jnp.float32)).astype(jnp.bfloat16)


class Copies:
    def __init__(self, sems):
        self.sems, self.count = sems, 0

    def __call__(self, source, target):
        copy = pltpu.make_async_copy(source, target, self.sems.at[self.count])
        self.count += 1
        copy.start()
        return copy


def copied_envs(copied, gathered, envs, shards_x, rows_d):
    return [
        copied(gathered.at[i, pl.ds(0, rows_d)], envs.at[pl.ds(i * rows_d, rows_d)]) for i in range(shards_x)
    ]


def rows_kernel(shards_x, rows_d, width, *refs):
    gathered, points = refs[0], refs[1:12]
    high_out, low_out = refs[12:14]
    envs, rows, high, low, sems = refs[14:]
    copied = Copies(sems)
    waits = copied_envs(copied, gathered, envs, shards_x, rows_d)
    place, ends = 0, []
    for point in points:
        size = point.shape[0]
        ends.append((place + size, copied(point, rows.at[pl.ds(place, size)])))
        place += size
    step = place // 3
    for copy in waits:
        copy.wait()
    waits, done = [], 0
    for m in range(3):
        while done < len(ends) and (done == 0 or ends[done - 1][0] < (m + 1) * step):
            ends[done][1].wait()
            done += 1
        part = pl.ds(m * step, step)
        value = dots_of(rows[part, :], envs[...])
        top, rest = two_parts(value * value / width)
        high[part, :] = top
        low[part, :] = rest
        waits += [copied(high.at[part], high_out.at[part]), copied(low.at[part], low_out.at[part])]
    for copy in waits:
        copy.wait()


def products_kernel(piece, shards_x, rows_d, width, env_count, core_ref, *refs):
    gathered, other, high_in, low_in = refs[:4]
    own_ref, send_ref = refs[4:6]
    envs, rows, high, low, dots, columns, both, sems = refs[6:]
    count = len(UNITS) * 2 * piece
    block = 2 * shards_x * piece
    at = 2 * block
    away = columns.shape[1] // 2
    copied = Copies(sems)
    waits = copied_envs(copied, gathered, envs, shards_x, rows_d)
    for i in range(shards_x):
        waits.append(copied(gathered.at[i, pl.ds(rows_d, 2 * piece)], rows.at[pl.ds(2 * i * piece, 2 * piece)]))
    waits.append(copied(other, rows.at[pl.ds(block, block)]))
    late = [copied(high_in, high), copied(low_in, low)]
    pick = (lax.broadcasted_iota(jnp.int32, (16, LANES), 1) == width) & (
        lax.broadcasted_iota(jnp.int32, (16, LANES), 0) == 0
    )
    rows[pl.ds(at, 16), :] = pick.astype(jnp.float32).astype(jnp.bfloat16)
    for copy in waits:
        copy.wait()

    dots[...] = dots_of(rows[...], envs[...])
    weights = dots[pl.ds(at, 8), :][:1] / env_count
    columns[...] = jnp.zeros_like(columns)
    for which in range(2):
        parts = []
        for low_y in range(2):
            for i in range(shards_x):
                value = dots[pl.ds(which * block + (2 * i + low_y) * piece, piece), :]
                parts.append(value * value / width * weights)
        top, rest = two_parts(jnp.concatenate(parts, axis=0))
        columns[0, pl.ds(which * away, block), :] = top
        columns[1, pl.ds(which * away, block), :] = rest
    for copy in late:
        copy.wait()

    step = count // 3

    def some_products(m, carry):
        part = pl.ds(pl.multiple_of(m * step, 16), step)
        both[part, :] = (
            dots_of(high[part, :], columns[0]) + dots_of(high[part, :], columns[1]) + dots_of(low[part, :], columns[0])
        )
        return carry

    lax.fori_loop(0, 3, some_products, 0)

    core = core_ref[0]
    for u, (distance, first_own) in enumerate(UNITS):
        for b in range(2):
            part = pl.ds((2 * u + b) * piece, piece)
            mine = first_own == (b == 0)
            ahead = 2 * distance + (0 if mine else 1)
            behind = (33 if mine else 32) - 2 * distance
            if ahead < 33:
                own_ref[ahead + core * (32 - 2 * ahead)] = both[part, pl.ds(0, block)]
            if behind < 33:
                send_ref[behind + (1 - core) * (32 - 2 * behind)] = both[part, pl.ds(away, block)]


def rows_call(gathered, points, rows_d, width):
    shards_x = gathered.shape[0]
    env_rows = shards_x * rows_d
    count = sum(p.shape[0] for p in points)
    shape = jax.ShapeDtypeStruct((count, env_rows), jnp.bfloat16)
    anywhere = pl.BlockSpec(memory_space=pl.ANY)
    return pl.pallas_call(
        functools.partial(rows_kernel, shards_x, rows_d, width),
        out_shape=(shape, shape),
        in_specs=[anywhere] * (1 + len(points)),
        out_specs=(anywhere, anywhere),
        scratch_shapes=[
            pltpu.VMEM((env_rows, LANES), jnp.bfloat16),
            pltpu.VMEM((count, LANES), jnp.bfloat16),
            pltpu.VMEM((count, env_rows), jnp.bfloat16),
            pltpu.VMEM((count, env_rows), jnp.bfloat16),
            pltpu.SemaphoreType.DMA((len(points) + shards_x + 6,)),
        ],
        compiler_params=pltpu.CompilerParams(vmem_limit_bytes=58 * 1024 * 1024),
        cost_estimate=pl.CostEstimate(
            flops=2 * env_rows * count * LANES, bytes_accessed=9 * 10**6, transcendentals=0
        ),
    )(gathered, *points)


def products_call(core, gathered, other, high, low, piece, rows_d, width, env_count):
    shards_x = gathered.shape[0]
    env_rows = shards_x * rows_d
    count = high.shape[0]
    block = 2 * shards_x * piece
    lanes = 2 * (-(-block // 128) * 128)
    shape = jax.ShapeDtypeStruct((33, piece, block), jnp.float32)
    anywhere = pl.BlockSpec(memory_space=pl.ANY)
    vmem = pl.BlockSpec(memory_space=pltpu.VMEM)
    return pl.pallas_call(
        functools.partial(products_kernel, piece, shards_x, rows_d, width, env_count),
        out_shape=(shape, shape),
        in_specs=[pl.BlockSpec(memory_space=pltpu.SMEM)] + [anywhere] * 4,
        out_specs=(vmem, vmem),
        scratch_shapes=[
            pltpu.VMEM((env_rows, LANES), jnp.bfloat16),
            pltpu.VMEM((2 * block + 16, LANES), jnp.bfloat16),
            pltpu.VMEM((count, env_rows), jnp.bfloat16),
            pltpu.VMEM((count, env_rows), jnp.bfloat16),
            pltpu.VMEM((2 * block + 16, env_rows), jnp.float32),
            pltpu.VMEM((2, lanes, env_rows), jnp.bfloat16),
            pltpu.VMEM((count, lanes), jnp.float32),
            pltpu.SemaphoreType.DMA((3 + 2 * shards_x,)),
        ],
        compiler_params=pltpu.CompilerParams(vmem_limit_bytes=58 * 1024 * 1024),
        cost_estimate=pl.CostEstimate(
            flops=2 * env_rows * (2 * block * LANES + 6 * count * block), bytes_accessed=9 * 10**6, transcendentals=0
        ),
    )(core, gathered, other, high, low)


def shards(descriptors, env_weights, sparse_points):
    core = lax.axis_index("wide") % 2
    narrow = lax.axis_size("narrow")
    wide = lax.axis_size("wide")
    shards_x = narrow // 2
    width = descriptors.shape[1]
    half = descriptors.shape[0] // 2
    env_count = descriptors.shape[0] * narrow
    piece = sparse_points.shape[0]

    mine = jnp.pad(sparse_points, ((0, 0), (0, LANES - width)))
    half_envs = lax.dynamic_slice_in_dim(
        jnp.concatenate(
            [descriptors, env_weights[:, None], jnp.zeros((2 * half, LANES - width - 1), descriptors.dtype)], axis=1
        ),
        core * half,
        half,
        0,
    )
    half_envs, mine = lax.optimization_barrier((half_envs, mine))
    across_envs = permuted(
        half_envs, lambda w, n: (w + (wide // 2 if w % 2 else 0), n + shards_x)
    )
    other = from_partner(mine)
    mine, other = lax.optimization_barrier((mine, other))
    four_mine = by_chips(mine, -4, -12)
    across_mine = permuted(mine, lambda w, n: (w, n + shards_x))
    unit = jnp.concatenate([mine, other], axis=0)
    at_zero = lax.axis_index("narrow") < shards_x
    payload = jnp.concatenate(
        [
            half_envs,
            across_envs,
            jnp.where(at_zero, mine, across_mine),
            jnp.where(at_zero, across_mine, mine),
        ],
        axis=0,
    )
    payload, unit, four_mine = lax.optimization_barrier((payload, unit, four_mine))
    groups = [list(range(shards_x)), list(range(shards_x, narrow))]
    gathered = lax.all_gather(payload, "narrow", axis=0, tiled=False, axis_index_groups=groups)

    def none(*_):
        return tuple(jnp.zeros((n * piece, LANES), unit.dtype) for n in (2, 2, 2, 2, 2, 4, 4, 4, 4, 4, 4))

    points = lax.cond(
        1 + jnp.minimum(lax.axis_index("wide"), 0) > 0,
        lambda *values: gather_wide(*values, core, piece),
        none,
        unit,
        four_mine,
    )
    gathered, points = lax.optimization_barrier((gathered, points))
    block_other = from_partner(gathered[:, 2 * half :].reshape(-1, LANES))
    high, low = rows_call(gathered, points, 2 * half, width)
    kept, sent = products_call(
        core.reshape(1), gathered, block_other, high, low, piece, 2 * half, width, env_count
    )
    return (kept + from_partner(sent))[None]


def solution(mesh):
    in_specs = (P("narrow", None), P("narrow"), P(("wide", "narrow"), None))
    out_specs = P("wide", None, "narrow", None)
    return jax.shard_map(shards, mesh=mesh, in_specs=in_specs, out_specs=out_specs, check_vma=False)
```

```python
import functools

import jax
import jax.numpy as jnp
from jax import lax
from jax.experimental import pallas as pl
from jax.experimental.pallas import tpu as pltpu
from jax.sharding import PartitionSpec as P

LANES = 2048
UNITS = (
    (0, True), (4, True), (8, True), (12, False), (16, True),
    (1, True), (5, True),
    (9, True), (7, True), (3, True), (13, False),
    (15, False), (11, False),
    (2, True), (6, True), (14, False), (10, False),
)


def permuted(value, move):
    wide, narrow = lax.axis_size("wide"), lax.axis_size("narrow")
    pairs = []
    for w in range(wide):
        for n in range(narrow):
            to_w, to_n = move(w, n)
            pairs.append((w * narrow + n, (to_w % wide) * narrow + to_n % narrow))
    return lax.ppermute(value, ("wide", "narrow"), pairs)


def by_chips(value, first, second):
    return permuted(value, lambda w, n: (w + 2 * (second if w % 2 else first), n))


def from_partner(value):
    return permuted(value, lambda w, n: (w ^ 1, n))


def gather_wide(unit, core, piece):
    four = by_chips(unit, -4, -12)
    sixteen_mine = by_chips(unit[:piece], -16, -16)
    sixteen = jnp.concatenate([sixteen_mine, from_partner(sixteen_mine)], axis=0)
    start = jnp.where(core == 0, unit, sixteen)
    stop = jnp.where(core == 0, sixteen, unit)
    near = by_chips(jnp.concatenate([start, four], axis=0), -1, 1)
    eight = by_chips(four[:piece], -4, 4)
    near, eight = lax.optimization_barrier((near, eight))
    two = by_chips(near, -1, 1)
    held = jnp.concatenate([four, eight], axis=0)
    back = by_chips(held, 1, -1)
    late = by_chips(eight, -1, 1)
    got = from_partner(held)
    far = from_partner(near)
    got_late = from_partner(jnp.concatenate([late, back], axis=0))
    two_far = from_partner(two)
    eights = jnp.concatenate([eight, got[2 * piece :]], axis=0)
    twelve = got[: 2 * piece]
    nines = jnp.concatenate([late, got_late[3 * piece :]], axis=0)
    sevens = jnp.concatenate([back[2 * piece :], got_late[:piece]], axis=0)
    threes, thirteens = back[: 2 * piece], got_late[piece : 3 * piece]
    return start, four, eights, twelve, stop, near, nines, sevens, threes, thirteens, far, two, two_far


def products_kernel(piece, shards_x, rows_d, tile, width, env_count, core_ref, *refs):
    gathered, points = refs[0], refs[1:14]
    own_ref, send_ref = refs[14:16]
    envs, rows, dots, columns, own, send, sems = refs[16:]
    count = len(UNITS) * 2 * piece
    block = 2 * shards_x * piece
    at = count + 4 * shards_x * piece
    tiles = envs.shape[0] // tile

    def copied(source, target):
        copies.append(pltpu.make_async_copy(source, target, sems.at[len(copies)]))
        copies[-1].start()
        return copies[-1]

    def copied_envs(i):
        return copied(gathered.at[i, pl.ds(0, rows_d)], envs.at[pl.ds(i * rows_d, rows_d)])

    copies, row_copies, sizes = [], [], []
    first = -(-tile // rows_d)
    env_copies = [copied_envs(i) for i in range(first)]
    place = 0
    for group in ((0, 1, 2, 3, 4), (5,), (6, 7, 8, 9), (10, 11, 12)):
        row_copies.append([])
        begin = place
        for k in group:
            size = points[k].shape[0]
            row_copies[-1].append(copied(points[k], rows.at[pl.ds(place, size)]))
            place += size
        sizes.append(place - begin)
    row_copies.append([])
    for i in range(shards_x):
        row_copies[-1].append(
            copied(gathered.at[i, pl.ds(rows_d, 4 * piece)], rows.at[pl.ds(place, 4 * piece)])
        )
        place += 4 * piece
    sizes.append(4 * shards_x * piece + 16)
    late_copies = [copied_envs(i) for i in range(first, shards_x)]
    pick = (lax.broadcasted_iota(jnp.int32, (16, LANES), 1) == width) & (
        lax.broadcasted_iota(jnp.int32, (16, LANES), 0) == 0
    )
    rows[pl.ds(at, 16), :] = pick.astype(jnp.float32).astype(jnp.bfloat16)

    def dots_of(part, t):
        dots[part, :] = lax.dot_general(
            rows[part, :],
            envs[pl.ds(t * tile, tile), :],
            (((1,), (1,)), ((), ())),
            preferred_element_type=jnp.float32,
        )

    step = rows.shape[0] // 4
    for t in range(tiles):
        if t == 0:
            for copy in env_copies:
                copy.wait()
            place = 0
            for waits, size in zip(row_copies, sizes):
                for copy in waits:
                    copy.wait()
                dots_of(pl.ds(place, size), 0)
                place += size
            for copy in late_copies:
                copy.wait()
        else:
            def some_dots(m, carry):
                dots_of(pl.ds(pl.multiple_of(m * step, 16), step), t)
                return carry

            lax.fori_loop(0, 4, some_dots, 0)
        weights = dots[pl.ds(at, 8), :][:1] / env_count
        for i in range(shards_x):
            for which in range(2):
                for low in range(2):
                    source = count + i * 4 * piece + (2 * which + low) * piece
                    target = which * block + (low * shards_x + i) * piece
                    value = dots[pl.ds(source, piece), :]
                    columns[pl.ds(target, piece), :] = value * value / width * weights
        high, low_part = [], []
        for which in range(2):
            value = columns[pl.ds(which * block, block), :]
            top = value.astype(jnp.bfloat16)
            high.append(top)
            low_part.append((value - top.astype(jnp.float32)).astype(jnp.bfloat16))

        def some_products(m, carry):
            part = pl.ds(pl.multiple_of(m * (count // 3), 8), count // 3)
            value = dots[part, :]
            value = value * value / width
            top = value.astype(jnp.bfloat16)
            rest = (value - top.astype(jnp.float32)).astype(jnp.bfloat16)
            for which, target in ((0, own), (1, send)):
                result = 0
                for left, right in ((top, high[which]), (top, low_part[which]), (rest, high[which])):
                    result += lax.dot_general(
                        left, right, (((1,), (1,)), ((), ())), preferred_element_type=jnp.float32
                    )
                target[part, :] = result if t == 0 else target[part, :] + result
            return carry

        lax.fori_loop(0, 3, some_products, 0)

    core = core_ref[0]
    for u, (distance, first_own) in enumerate(UNITS):
        for b in range(2):
            part = pl.ds((2 * u + b) * piece, piece)
            mine = first_own == (b == 0)
            ahead = 2 * distance + (0 if mine else 1)
            behind = (33 if mine else 32) - 2 * distance
            if ahead < 33:
                own_ref[ahead + core * (32 - 2 * ahead)] = own[part, :]
            if behind < 33:
                send_ref[behind + (1 - core) * (32 - 2 * behind)] = send[part, :]


def products(core, gathered, points, piece, rows_d, width, env_count):
    shards_x = gathered.shape[0]
    env_rows = shards_x * rows_d
    tile = 256 if env_rows % 256 == 0 else env_rows
    count = len(UNITS) * 2 * piece
    block = 2 * shards_x * piece
    total = count + 4 * shards_x * piece + 16
    shape = jax.ShapeDtypeStruct((33, piece, block), jnp.float32)
    anywhere = pl.BlockSpec(memory_space=pl.ANY)
    vmem = pl.BlockSpec(memory_space=pltpu.VMEM)
    flops = 2 * env_rows * (total * LANES + 6 * count * block)
    return pl.pallas_call(
        functools.partial(products_kernel, piece, shards_x, rows_d, tile, width, env_count),
        out_shape=(shape, shape),
        in_specs=[pl.BlockSpec(memory_space=pltpu.SMEM)] + [anywhere] * (1 + len(points)),
        out_specs=(vmem, vmem),
        scratch_shapes=[
            pltpu.VMEM((env_rows, LANES), jnp.bfloat16),
            pltpu.VMEM((total, LANES), jnp.bfloat16),
            pltpu.VMEM((total, tile), jnp.float32),
            pltpu.VMEM((2 * block, tile), jnp.float32),
            pltpu.VMEM((count, block), jnp.float32),
            pltpu.VMEM((count, block), jnp.float32),
            pltpu.SemaphoreType.DMA((len(points) + 2 * shards_x,)),
        ],
        compiler_params=pltpu.CompilerParams(vmem_limit_bytes=40 * 1024 * 1024),
        cost_estimate=pl.CostEstimate(flops=flops, bytes_accessed=10**7, transcendentals=0),
    )(core, gathered, *points)


def shards(descriptors, env_weights, sparse_points):
    core = lax.axis_index("wide") % 2
    narrow = lax.axis_size("narrow")
    wide = lax.axis_size("wide")
    shards_x = narrow // 2
    width = descriptors.shape[1]
    half = descriptors.shape[0] // 2
    env_count = descriptors.shape[0] * narrow
    piece = sparse_points.shape[0]

    mine = jnp.pad(sparse_points, ((0, 0), (0, LANES - width)))
    other = from_partner(mine)
    across_mine = permuted(mine, lambda w, n: (w, n + shards_x))
    unit = jnp.concatenate([mine, other], axis=0)
    half_envs = lax.dynamic_slice_in_dim(
        jnp.concatenate(
            [descriptors, env_weights[:, None], jnp.zeros((2 * half, LANES - width - 1), descriptors.dtype)], axis=1
        ),
        core * half,
        half,
        0,
    )
    across_envs = permuted(
        half_envs, lambda w, n: (w + (wide // 2 if w % 2 else 0), n + shards_x)
    )
    across_other = from_partner(across_mine)
    at_zero = lax.axis_index("narrow") < shards_x
    payload = jnp.concatenate(
        [
            half_envs,
            across_envs,
            jnp.where(at_zero, mine, across_mine),
            jnp.where(at_zero, across_mine, mine),
            jnp.where(at_zero, other, across_other),
            jnp.where(at_zero, across_other, other),
        ],
        axis=0,
    )
    payload, unit = lax.optimization_barrier((payload, unit))
    groups = [list(range(shards_x)), list(range(shards_x, narrow))]
    gathered = lax.all_gather(payload, "narrow", axis=0, tiled=False, axis_index_groups=groups)

    def none(*_):
        return tuple(jnp.zeros((n * piece, LANES), unit.dtype) for n in (2, 2, 2, 2, 2, 4, 2, 2, 2, 2, 4, 4, 4))

    points = lax.cond(
        1 + jnp.minimum(lax.axis_index("wide"), 0) > 0,
        lambda *values: gather_wide(*values, core, piece),
        none,
        unit,
    )
    gathered, points = lax.optimization_barrier((gathered, points))
    kept, sent = products(core.reshape(1), gathered, points, piece, 2 * half, width, env_count)
    return (kept + from_partner(sent))[None]


def solution(mesh):
    in_specs = (P("narrow", None), P("narrow"), P(("wide", "narrow"), None))
    out_specs = P("wide", None, "narrow", None)
    return jax.shard_map(shards, mesh=mesh, in_specs=in_specs, out_specs=out_specs, check_vma=False)
```
